512 devices in a mesh: row: 32 (over z, core), col: 16 (over y, x).
Axes of the slice: x: 4, y: 4, z: 16, core: 2. Of those that a mesh axis runs over, the one named last changes fastest.
Arguments:
- rhs: float32 [32, 1024, 4096], P('row', None, 'col'), may hold values from -6 to 6
- panel: float32 [32, 2, 1024, 1024], P('row', None, 'col'), may hold values from -0.125 to 0.125
- diag_inverse: float32 [2, 1024, 1024], P(None, 'row'), as said below
- flags: int32 [32, 2], P('row'), may hold values 0 or 1
- slot_block: int32 [32], replicated, may hold values from 0 to 31, each once
Outputs:
- result: float32 [32, 1024, 4096], P('row', None, 'col')
The draws below stay inside these ranges and needn't reach their ends.
Inputs may be any that keep to these rules, and one draw needn't show every extreme that they name: `slot_block`: each block row 0 to 31 is held by exactly one slot. `diag_inverse`: lower triangular with a positive diagonal.
All inputs are finite; a program needn't handle non-finite values. No bound on the sum of `flags` on one device may be relied on, other than what follows from the above.
Results may differ from the reference program's by a relative error of at most 0.000078.
Values sent between devices are 32-bit elements; how exact they have to be, the bound alone decides.
A program may use at most 64 MiB of HBM per device.

```python
import math
import jax
import jax.numpy as jnp
from jax import lax

NB = 1024
NBLK = 32
NRHS = 4096


def draw_diag_inverse(key, part):
    key = jax.random.fold_in(key, 5)
    key_low, key_diag = jax.random.split(key)
    rows = lax.broadcasted_iota(jnp.int32, (2, NB, NB), 1)
    cols = lax.broadcasted_iota(jnp.int32, (2, NB, NB), 2)
    lower = jax.random.normal(key_low, (2, NB, NB), jnp.float32) * (1.5 / math.sqrt(NB))
    middle = jax.random.uniform(key_diag, (2, NB, NB), jnp.float32, 1.0, 2.0)
    return jnp.where(rows > cols, lower, jnp.where(rows == cols, middle, 0.0)).astype(jnp.float32)


def touch_ends(result, stream_key, low, top_value):
    spot = [jax.random.randint(jax.random.fold_in(stream_key, axis), (), 0, length) for axis, length in enumerate(result.shape)]
    main_axis = result.shape.index(max(result.shape))
    next_to = spot[:main_axis] + [(spot[main_axis] + 1) % result.shape[main_axis]] + spot[main_axis + 1:]
    return result.at[tuple(spot)].set(low).at[tuple(next_to)].set(top_value)


def block_levels(own_key, extent, pieces, least, high):
    def one(position, shards_of):
        draws = jax.random.uniform(jax.random.fold_in(jax.random.fold_in(own_key, 6), position), (shards_of,), jnp.float32, least / len(pieces), high / len(pieces))
        return jnp.repeat(jnp.exp(draws), extent[position] // shards_of).reshape((-1,) + (1,) * (len(extent) - position - 1))

    gain = one(*pieces[0])
    for cut in pieces[1:]:
        gain = gain * one(*cut)
    return gain


def scatter_about(key, extent, width, reach, cuts=(), dtype=jnp.bfloat16):
    values = width * jax.random.normal(key, extent, jnp.float32)
    if cuts:
        values = values * block_levels(key, extent, cuts, -0.22, 0.18)
    return jnp.clip(values, -reach, reach).astype(dtype)


def setup_inputs(seed: int = 0) -> dict:
    arg_keys = jax.random.split(jax.random.key(seed), 6)
    rhs = scatter_about(arg_keys[0], (NBLK, NB, NRHS), 1.0, 6.0, ((0, 32), (2, 16)), jnp.float32)
    panel = scatter_about(arg_keys[1], (NBLK, 2, NB, NB), (2 * NB) ** -0.5, 0.125, ((0, 32), (2, 16)), jnp.float32)
    diag_inverse = draw_diag_inverse(jax.random.fold_in(arg_keys[5], 71), 0)
    flags = touch_ends((jax.random.randint(arg_keys[3], (NBLK, 2), 0, 4) < 3).astype(jnp.int32), jax.random.fold_in(arg_keys[3], 1), 0, 1)
    slot_block = jax.random.permutation(arg_keys[4], NBLK).astype(jnp.int32)
    return {"rhs": rhs, "panel": panel, "diag_inverse": diag_inverse, "flags": flags, "slot_block": slot_block}


def reference(rhs, panel, diag_inverse, flags, slot_block):
    highest = lax.Precision.HIGHEST
    weights = flags.astype(jnp.float32)
    slot_zero = jnp.argmax(slot_block == 0).astype(jnp.int32)
    slot_one = jnp.argmax(slot_block == 1).astype(jnp.int32)
    solved0 = jnp.dot(diag_inverse[0], rhs[slot_zero], precision=highest)
    first = rhs - weights[:, 0][:, None, None] * jnp.einsum("sij,jr->sir", panel[:, 0], solved0, precision=highest)
    solved1 = jnp.dot(diag_inverse[1], first[slot_one], precision=highest)
    second = first - weights[:, 1][:, None, None] * jnp.einsum("sij,jr->sir", panel[:, 1], solved1, precision=highest)
    is_zero = (slot_block == 0)[:, None, None]
    is_one = (slot_block == 1)[:, None, None]
    return jnp.where(is_zero, solved0[None], jnp.where(is_one, solved1[None], second))
```

```python
import jax
import jax.numpy as jnp
from jax import lax
from jax.experimental import pallas as pl
from jax.experimental.pallas import tpu as pltpu
from jax.sharding import PartitionSpec as P

MESH = pl.DeviceIdType.MESH
F32 = jnp.float32
BF16 = jnp.bfloat16
Z = 16
S = 4


def split(a):
    high = a.astype(BF16)
    return high, (a - high.astype(F32)).astype(BF16)


def dot(a, b):
    return jnp.dot(a, b, preferred_element_type=F32)


def dot3(a, b_high, b_low):
    a_high, a_low = split(a)
    return dot(a_high, b_high) + (dot(a_high, b_low) + dot(a_low, b_high))


class Copy:
    def __init__(self, make):
        self.make = make

    def op(self):
        src, dst, send, recv, device = self.make()
        return pltpu.make_async_remote_copy(
            src_ref=src, dst_ref=dst, send_sem=send, recv_sem=recv, device_id=device, device_id_type=MESH
        )

    def start(self):
        self.op().start()

    def sent(self):
        self.op().wait_send()

    def came(self):
        self.op().wait_recv()


class Plane:
    def __init__(self, place, a, b, send, recv, base=0):
        self.r, self.y, self.x = place
        self.a, self.b, self.send, self.recv, self.base = a, b, send, recv, base
        self.sends = []

    def copy(self, n, piece, place, dx, dy):
        def make():
            y, x = lax.rem(self.y + dy + S, S), lax.rem(self.x + dx + S, S)
            view = piece(*self.at(*place))
            return view, view, self.send.at[self.base + n], self.recv.at[self.base + n], (self.r, y * S + x)
        return Copy(make)

    def at(self, dy, dx, part):
        y = None if dy is None else lax.rem(self.y + dy, S)
        x = None if dx is None else lax.rem(self.x + dx, S)
        return y, x, part

    def put(self, n, piece, place, dx, dy):
        copy = self.copy(n, piece, place, dx, dy)
        copy.start()
        self.sends.append(copy)

    def got(self, n, piece, place):
        self.copy(n, piece, place, 0, 0).came()

    def a0(self):
        self.put(0, self.a, (0, 0, 0), 1, 0)
        self.put(1, self.a, (0, 0, 0), -1, 0)
        self.put(2, self.b, (0, 0, 0), 0, 1)
        self.put(3, self.b, (0, 0, 0), 0, -1)

    def a1(self):
        self.got(0, self.a, (0, 3, 0))
        self.put(4, self.a, (0, 3, 1), 1, 0)
        self.got(2, self.b, (3, 0, 0))
        self.put(6, self.b, (3, 0, 1), 0, 1)
        self.got(1, self.a, (0, 1, 0))
        self.put(5, self.a, (0, 1, 2), -1, 0)
        self.got(3, self.b, (1, 0, 0))
        self.put(7, self.b, (1, 0, 2), 0, -1)

    def b0(self):
        self.got(4, self.a, (0, 2, 1))
        self.got(5, self.a, (0, 2, 2))
        self.put(8, self.a, (0, None, 0), 0, 1)
        self.put(9, self.a, (0, None, 0), 0, -1)
        self.got(6, self.b, (2, 0, 1))
        self.got(7, self.b, (2, 0, 2))
        self.put(10, self.b, (None, 0, 0), 1, 0)
        self.put(11, self.b, (None, 0, 0), -1, 0)

    def b1(self):
        self.got(8, self.a, (3, None, 0))
        self.put(12, self.a, (3, None, 1), 0, 1)
        self.got(10, self.b, (None, 3, 0))
        self.put(14, self.b, (None, 3, 1), 1, 0)
        self.got(9, self.a, (1, None, 0))
        self.put(13, self.a, (1, None, 2), 0, -1)
        self.got(11, self.b, (None, 1, 0))
        self.put(15, self.b, (None, 1, 2), -1, 0)

    def end(self):
        self.got(12, self.a, (2, None, 1))
        self.got(13, self.a, (2, None, 2))
        self.got(14, self.b, (None, 2, 1))
        self.got(15, self.b, (None, 2, 2))

    def sent(self):
        for copy in self.sends:
            copy.sent()


class Gather:
    def __init__(self, z, q, c, buf, send, recv):
        self.z, self.q, self.c, self.buf, self.send, self.recv = z, q, c, buf, send, recv
        self.sends = []

    def copy(self, n, chunk, dz):
        def make():
            to = lax.rem(self.z + dz + Z, Z)
            view = self.buf.at[lax.rem(self.z + chunk + Z, Z)]
            return view, view, self.send.at[n], self.recv.at[n], (to * 2 + self.q, self.c)
        return Copy(make)

    def put(self, n, chunk, dz):
        copy = self.copy(n, chunk, dz)
        copy.start()
        self.sends.append(copy)

    def got(self, n, chunk):
        self.copy(n, chunk, 0).came()

    def first(self):
        self.put(0, 0, 2)
        self.put(8, 0, -2)
        self.put(4, 0, 1)
        self.put(11, 0, -1)

    def step(self, k):
        self.got(k - 1, -2 * k)
        self.put(k, -2 * k, 2)
        self.put(4 + k, -2 * k, 1)
        self.got(8 + k - 1, 2 * k)
        if k < 3:
            self.put(8 + k, 2 * k, -2)
        self.put(11 + k, 2 * k, -1)

    def end(self):
        self.got(3, -8)
        for k in range(4):
            self.got(4 + k, -2 * k - 1)
            self.got(11 + k, 2 * k + 1)

    def sent(self):
        for copy in self.sends:
            copy.sent()


def kernel(
    slot_ref, flag_ref, rhs_ref, panel_ref, diag_ref, out_ref,
    full, low, mine0, other0, mine1, other1, even_r, odd_r, even_l, odd_l, hop_r, hop_l,
    ez, ea, eb, ea0, eb0, p10, b0, b1c, b1, x0, x1, xh, xl, wh, wl,
    p_send, p_recv, e_send, e_recv, t_send, t_recv, r0_send, r0_recv, g0_send, g0_recv,
    r1_send, r1_recv, g1_send, g1_recv, m_send, m_recv, z_send, z_recv, z_self, f_send, f_recv,
):
    r, c = lax.axis_index("row"), lax.axis_index("col")
    z, q = r // 2, lax.rem(r, 2)
    y, x = c // S, lax.rem(c, S)
    pair = (z * 2 + 1 - q, c)

    def turn(a, n):
        return lax.rem(a + 2 * n, n)

    barrier = pltpu.get_barrier_semaphore()

    def hello(device):
        pl.semaphore_signal(barrier, inc=1, device_id=device, device_id_type=MESH)

    for dy, dx in ((0, 1), (0, -1), (1, 0), (-1, 0)):
        hello((r, turn(y + dy, S) * S + turn(x + dx, S)))
    hello(pair)
    for d in (1, 2, 3, 4):
        for dz in (d, -d):
            for core in range(2):
                hello((turn(z + dz, Z) * 2 + core, c))

    held = slot_ref[r]
    is0 = jnp.where(held == 0, 1.0, 0.0).astype(F32)
    is1 = jnp.where(held == 1, 1.0, 0.0).astype(F32)
    f0 = flag_ref[0, 0].astype(F32)
    f1 = flag_ref[0, 1].astype(F32)

    def keep(mark, a, b):
        return jnp.where(jnp.full(a.shape, mark, F32) > 0.5, a, b)

    def mask0(d, _):
        j = lax.rem(z + d, Z)
        rows = rhs_ref[pl.ds(pl.multiple_of(j * 64, 64), 64), :]
        mine0[d, 0:64, :] = keep(is0, rows, jnp.zeros_like(rows))
        t = j // 2
        block = panel_ref[0, pl.ds(pl.multiple_of(t * 8, 8), 8), :] * f0
        block = keep(is1, block, jnp.zeros_like(block))
        for a in range(4):
            mine0[d, 64 + 8 * a : 72 + 8 * a, :] = block[:, 256 * a : 256 * a + 256]
        return 0

    def mask1(d, _):
        j = lax.rem(z + d, Z)
        t, h = j // 2, lax.rem(j, 2)
        for k in range(16):
            rows = rhs_ref[pl.ds(pl.multiple_of(64 * k + t * 8, 8), 8), pl.ds(pl.multiple_of(h * 128, 128), 128)]
            mine1[d, 8 * k : 8 * k + 8, :] = keep(is1, rows, jnp.zeros_like(rows))
        return 0

    lax.fori_loop(0, Z, mask0, 0)
    for k in range(2):
        full[k, y, x] = panel_ref[k]

    pl.semaphore_wait(barrier, 21)

    place = (r, y, x)

    def half(lo, hi):
        def view(k):
            def piece(yy, xx, part):
                mid = (lo + hi) // 2
                rows = pl.ds(*((lo, hi - lo), (lo, mid - lo), (mid, hi - mid))[part])
                yy = slice(None) if yy is None else yy
                xx = slice(None) if xx is None else xx
                return full.at[k, yy, xx, rows, :]
            return piece
        return view

    top, bottom = half(0, 32), half(32, 64)
    panels = [Plane(place, top(k), bottom(k), p_send, p_recv, 16 * k) for k in range(2)]

    def columns(buf, lo, hi):
        def piece(yy, xx, part):
            mid = (lo + hi) // 2
            cols = pl.ds(*((lo, hi - lo), (lo, mid - lo), (mid, hi - mid))[part])
            yy = slice(None) if yy is None else yy
            xx = slice(None) if xx is None else xx
            return buf.at[yy, xx, :, cols]
        return piece

    diag = Plane(place, columns(ea, 0, 2560), columns(eb, 0, 2560), e_send, e_recv)
    tenth = Plane(place, columns(p10, 0, 512), columns(p10, 512, 1024), t_send, t_recv)
    gather0 = Gather(z, q, c, b0, g0_send, g0_recv)
    gather1 = Gather(z, q, c, b1c, g1_send, g1_recv)

    panels[0].a0()

    groups = ((6, 5), (11, 5), (0, 6))
    merges = [
        Copy(lambda i=i, g=g: (mine0.at[pl.ds(*g)], other0.at[pl.ds(*g)], m_send.at[i], m_recv.at[i], pair))
        for i, g in enumerate(groups)
    ]
    merges.append(Copy(lambda: (mine1, other1, m_send.at[3], m_recv.at[3], pair)))

    @pl.when(q == 0)
    def _():
        for copy in merges[:3]:
            copy.start()

    lax.fori_loop(0, Z, mask1, 0)

    @pl.when(q == 0)
    def _():
        merges[3].start()

    reduce0 = []
    reduce1 = []

    def send0(n, d, to, buf, i):
        copy = Copy(lambda: (mine0.at[d % Z], buf.at[i], r0_send.at[n], r0_recv.at[n], (turn(z + to, Z) * 2 + q, c)))
        copy.start()
        reduce0.append(copy)

    def recv0(n, buf, i):
        Copy(lambda: (buf.at[i], buf.at[i], r0_send.at[n], r0_recv.at[n], (r, c))).came()

    def merge0(i):
        merges[i].came()
        lo, n = groups[i]
        for d in range(lo, lo + n):
            mine0[d] += other0[d]

    def send1(n, d, to, buf, i):
        copy = Copy(lambda: (mine1.at[d % Z], buf.at[i], r1_send.at[n], r1_recv.at[n], (turn(z + to, Z) * 2 + q, c)))
        copy.start()
        reduce1.append(copy)

    def recv1(n, buf, i):
        Copy(lambda: (buf.at[i], buf.at[i], r1_send.at[n], r1_recv.at[n], (r, c))).came()

    def hop(t):
        if t:
            recv1(t - 1, hop_r, t - 1)
            mine1[8 - t] += hop_r[t - 1]
        if t < 8:
            send1(t, 8 - t, 1, hop_r, t)
        if 0 < t < 8:
            recv1(8 + t - 1, hop_l, t - 1)
            mine1[(t - 7) % Z] += hop_l[t - 1]
        if t < 7:
            send1(8 + t, t - 7, -1, hop_l, t)

    @pl.when(q == 1)
    def _():
        merge0(0)
        send0(0, 8, 2, even_r, 0)
        send0(4, 7, 1, odd_r, 0)
        send0(11, -7, -1, odd_l, 0)
        merge0(1)
        merge0(2)
        for i, d in ((1, 5), (2, 3), (3, 1)):
            send0(4 + i, d, 1, odd_r, i)
            send0(11 + i, -d, -1, odd_l, i)
        recv0(11, odd_l, 0)
        mine0[10] += odd_l[0]
        send0(8, -6, -2, even_l, 0)

    fold = (z // 2 + 1) // 2
    target = lax.rem(fold, 2)
    slot = z // 4
    holds = jnp.logical_and(lax.rem(z, 2) == c // 8, q == lax.rem(c // 4, 2))
    def rows():
        return diag_ref.at[:, pl.ds(pl.multiple_of(lax.rem(c, 4) * 8, 8), 8), :]

    spread = []
    for n, dz in enumerate((4, -4, 3, -3, 2, -2, 1, -1)):
        spread.append(Copy(lambda n=n, dz=dz: (rows(), ez.at[slot], z_send.at[n], z_recv.at[slot], (turn(z + dz, Z) * 2 + target, c))))
    across = Copy(lambda: (rows(), ez.at[slot], z_send.at[8], z_recv.at[slot], pair))

    @pl.when(holds)
    def _():
        for copy in spread:
            copy.start()

        @pl.when(target == q)
        def _():
            pltpu.make_async_copy(rows(), ez.at[slot], z_recv.at[slot]).start()

        @pl.when(target != q)
        def _():
            across.start()

    panels[1].a0()

    @pl.when(q == 1)
    def _():
        recv0(0, even_r, 0)
        recv0(4, odd_r, 0)
        mine0[6] += even_r[0] + odd_r[0]
        send0(1, 6, 2, even_r, 1)
        recv0(8, even_l, 0)
        recv0(12, odd_l, 1)
        mine0[12] += even_l[0] + odd_l[1]
        send0(9, -4, -2, even_l, 1)
        merges[3].came()
        mine1[...] += other1[...]
        hop(0)

    panels[0].a1()

    def wait_slot(m):
        Copy(lambda: (ez.at[m], ez.at[m], z_send.at[0], z_recv.at[m], (r, c))).came()

    relays = []
    for base, step, reach in ((9, 1, (4, 3, 2, 1)), (13, -1, (3, 2, 1))):
        origin = turn(z - 4 * step, Z)
        serves = jnp.logical_and(lax.rem(origin, 2) == c // 8, lax.rem((origin // 2 + 1) // 2, 2) == q)
        m = origin // 4
        copies = [
            Copy(lambda n=base + i, m=m, dz=step * d: (ez.at[m], ez.at[m], z_send.at[n], z_recv.at[m], (turn(z + dz, Z) * 2 + q, c)))
            for i, d in enumerate(reach)
        ]
        relays.append((serves, copies))

        @pl.when(serves)
        def _(m=m, copies=copies):
            wait_slot(m)
            for copy in copies:
                copy.start()

    @pl.when(q == 1)
    def _():
        recv0(1, even_r, 1)
        recv0(5, odd_r, 1)
        mine0[4] += even_r[1] + odd_r[1]
        send0(2, 4, 2, even_r, 2)
        recv0(9, even_l, 1)
        recv0(13, odd_l, 2)
        mine0[14] += even_l[1] + odd_l[2]
        send0(10, -2, -2, even_l, 2)
        hop(1)

    panels[0].b0()

    for m in range(4):
        origin = 2 * (2 * m + lax.rem(q + m, 2)) + c // 8
        away = turn(origin - z, Z)
        waited = jnp.logical_or(away == 4, away == 12)

        @pl.when(jnp.logical_not(waited))
        def _(m=m):
            wait_slot(m)

    for k in range(2):
        o = 1280 * k
        ea[y, x, :, o : o + 256] = ez[0, k, :, 0:256]
        ea[y, x, :, o + 256 : o + 1280] = ez[3, k, :, :]
        eb[y, x, :, o : o + 512] = ez[1, k, :, 0:512]
        eb[y, x, :, o + 512 : o + 1280] = ez[2, k, :, 0:768]
    diag.a0()

    @pl.when(q == 1)
    def _():
        recv0(2, even_r, 2)
        recv0(6, odd_r, 2)
        mine0[2] += even_r[2] + odd_r[2]
        send0(3, 2, 2, even_r, 3)
        hop(2)

    panels[1].a1()

    @pl.when(q == 1)
    def _():
        recv0(3, even_r, 3)
        recv0(7, odd_r, 3)
        recv0(10, even_l, 2)
        recv0(14, odd_l, 3)
        total = mine0[0] + ((even_r[3] + odd_r[3]) + (even_l[2] + odd_l[3]))
        b0[z] = total[0:64]
        gather0.first()
        for a in range(4):
            p10[y, x, :, 256 * a : 256 * a + 256] = total[64 + 8 * a : 72 + 8 * a]
        tenth.a0()
        hop(3)

    diag.a1()

    @pl.when(q == 1)
    def _():
        gather0.step(1)
        tenth.a1()
        hop(4)

    diag.b0()
    panels[0].b1()

    @pl.when(q == 1)
    def _():
        gather0.step(2)
        tenth.b0()
        hop(5)

    diag.b1()

    @pl.when(q == 1)
    def _():
        gather0.step(3)
        tenth.b1()
        hop(6)

    panels[1].b0()
    panels[0].end()
    diag.end()

    def put_pair(n, src, dst):
        return Copy(lambda: (src, dst, f_send.at[n], f_recv.at[n], pair))

    gifts = [put_pair(0, ea, ea0), put_pair(1, eb, eb0)]

    @pl.when(q == 0)
    def _():
        for copy in gifts:
            copy.start()

    first = [put_pair(2, x0, x0)]
    second = [put_pair(3 + i, x1.at[pl.ds(256 * i, 256)], x1.at[pl.ds(256 * i, 256)]) for i in range(4)]

    def solve(step, source, target_ref, after):
        for b in range(8):
            m, core = b // 2, (b // 2 + b) % 2
            buf, base = (((ea0, ea), 0), ((eb0, eb), 0), ((eb0, eb), 512), ((ea0, ea), 256))[m]
            base += 1280 * step
            width = 128 * (b + 1)
            part = buf[core][:, :, :, base : base + width].reshape(128, width)
            target_ref[128 * b : 128 * b + 128, :] = dot3(part, xh[0:width, :], xl[0:width, :])
            after(b)

    def take(ref):
        for i in range(4):
            high, low_part = split(ref[256 * i : 256 * i + 256, :])
            xh[256 * i : 256 * i + 256, :] = high
            xl[256 * i : 256 * i + 256, :] = low_part

    @pl.when(q == 1)
    def _():
        gather0.end()
        for i in range(16):
            high, low_part = split(b0[i])
            xh[64 * i : 64 * i + 64, :] = high
            xl[64 * i : 64 * i + 64, :] = low_part
        for copy in gifts:
            copy.came()
        solve(0, b0, x0, lambda b: None)
        first[0].start()
        take(x0)
        tenth.end()
        hop(7)
        hop(8)
        h = pl.multiple_of(lax.rem(z, 2) * 128, 128)
        rows1 = mine1[0]
        product = dot3(p10[...].reshape(128, 1024), xh[:, pl.ds(h, 128)], xl[:, pl.ds(h, 128)])
        b1c[z] = rows1 - product
        gather1.first()

    @pl.when(q == 0)
    def _():
        first[0].came()
        take(x0)

    def piece0(i):
        rows_ = slice(256 * i, 256 * i + 256)
        product = dot3(full[0, i].reshape(256, 1024), xh[...], xl[...])
        out_ref[rows_, :] = rhs_ref[rows_, :] - f0 * product

    piece0(0)

    @pl.when(q == 1)
    def _():
        gather1.step(1)

    panels[1].b1()
    piece0(1)

    @pl.when(q == 1)
    def _():
        gather1.step(2)

    piece0(2)

    @pl.when(q == 1)
    def _():
        gather1.step(3)

    piece0(3)
    panels[1].end()

    def split_panel(i):
        high, low_part = split(full[1, i].reshape(256, 1024))
        wh[256 * i : 256 * i + 256, :] = high
        wl[256 * i : 256 * i + 256, :] = low_part

    for i in range(4):
        split_panel(i)

    @pl.when(q == 1)
    def _():
        gather1.end()
        for t in range(8):
            for h in range(2):
                for k in range(16):
                    b1[64 * k + 8 * t : 64 * k + 8 * t + 8, 128 * h : 128 * h + 128] = b1c[2 * t + h, 8 * k : 8 * k + 8, :]
        take(b1)

        def after(b):
            if b % 2:
                second[b // 2].start()

        solve(1, b1, x1, after)

    @pl.when(q == 0)
    def _():
        for copy in second:
            copy.came()

    take(x1)
    for i in range(4):
        rows_ = slice(256 * i, 256 * i + 256)
        product = dot(wh[rows_, :], xh[...]) + (dot(wh[rows_, :], xl[...]) + dot(wl[rows_, :], xh[...]))
        value = out_ref[rows_, :] - f1 * product
        out_ref[rows_, :] = keep(is0, x0[rows_, :], keep(is1, x1[rows_, :], value))

    for gather in panels + [diag]:
        gather.sent()

    @pl.when(q == 0)
    def _():
        for copy in merges + gifts:
            copy.sent()

    @pl.when(q == 1)
    def _():
        tenth.sent()
        for copy in reduce0 + reduce1 + first + second:
            copy.sent()
        gather0.sent()
        gather1.sent()

    @pl.when(holds)
    def _():
        for copy in spread:
            copy.sent()

        @pl.when(target != q)
        def _():
            across.sent()

    for serves, copies in relays:

        @pl.when(serves)
        def _(copies=copies):
            for copy in copies:
                copy.sent()


def shards(rhs, panel, diag_inverse, flags, slot_block):
    vmem = lambda *shape, dtype=F32: pltpu.VMEM(shape, dtype)
    dma = lambda *shape: pltpu.SemaphoreType.DMA(shape)
    scratch = [
        vmem(2, 4, 4, 64, 1024),
        vmem(8, 128),
        vmem(16, 96, 256),
        vmem(16, 96, 256),
        vmem(16, 128, 128),
        vmem(16, 128, 128),
        vmem(4, 96, 256),
        vmem(4, 96, 256),
        vmem(3, 96, 256),
        vmem(4, 96, 256),
        vmem(8, 128, 128),
        vmem(7, 128, 128),
        vmem(4, 2, 8, 1024),
        vmem(4, 4, 8, 2560),
        vmem(4, 4, 8, 2560),
        vmem(4, 4, 8, 2560),
        vmem(4, 4, 8, 2560),
        vmem(4, 4, 8, 1024),
        vmem(16, 64, 256),
        vmem(16, 128, 128),
        vmem(1024, 256),
        vmem(1024, 256),
        vmem(1024, 256),
        vmem(1024, 256, dtype=BF16),
        vmem(1024, 256, dtype=BF16),
        vmem(1024, 1024, dtype=BF16),
        vmem(1024, 1024, dtype=BF16),
        dma(32), dma(32), dma(16), dma(16), dma(16), dma(16),
        dma(15), dma(15), dma(15), dma(15),
        dma(15), dma(15), dma(15), dma(15),
        dma(4), dma(4), dma(16), dma(4), dma(1), dma(7), dma(7),
    ]
    whole = pl.BlockSpec(memory_space=pltpu.VMEM)
    scalar = pl.BlockSpec(memory_space=pltpu.SMEM)
    result = pl.pallas_call(
        kernel,
        out_shape=jax.ShapeDtypeStruct((1024, 256), F32),
        in_specs=[scalar, scalar, whole, whole, whole],
        out_specs=whole,
        scratch_shapes=scratch,
        name="substitution",
        compiler_params=pltpu.CompilerParams(collective_id=0, has_side_effects=True, vmem_limit_bytes=56 << 20),
    )(slot_block, flags, rhs[0], panel[0], diag_inverse)
    return result[None]


def solution(mesh):
    in_specs = (
        P("row", None, "col"),
        P("row", None, "col", None),
        P(None, "row", None),
        P("row", None),
        P(),
    )
    out_specs = P("row", None, "col")
    return jax.shard_map(shards, mesh=mesh, in_specs=in_specs, out_specs=out_specs, check_vma=False)
```

```python
import jax
import jax.numpy as jnp
from jax import lax
from jax.experimental import pallas as pl
from jax.experimental.pallas import tpu as pltpu
from jax.sharding import PartitionSpec as P

MESH = pl.DeviceIdType.MESH
F32 = jnp.float32
BF16 = jnp.bfloat16
Z = 16
S = 4


def split(a):
    high = a.astype(BF16)
    return high, (a - high.astype(F32)).astype(BF16)


def dot(a, b):
    return jnp.dot(a, b, preferred_element_type=F32)


def dot3(a, b_high, b_low):
    a_high, a_low = split(a)
    return dot(a_high, b_high) + (dot(a_high, b_low) + dot(a_low, b_high))


class Copy:
    def __init__(self, make):
        self.make = make

    def op(self):
        src, dst, send, recv, device = self.make()
        return pltpu.make_async_remote_copy(
            src_ref=src, dst_ref=dst, send_sem=send, recv_sem=recv, device_id=device, device_id_type=MESH
        )

    def start(self):
        self.op().start()

    def sent(self):
        self.op().wait_send()

    def came(self):
        self.op().wait_recv()


class Plane:
    def __init__(self, place, a, b, send, recv, base=0):
        self.r, self.y, self.x = place
        self.a, self.b, self.send, self.recv, self.base = a, b, send, recv, base
        self.sends = []

    def copy(self, n, piece, place, dx, dy):
        def make():
            y, x = lax.rem(self.y + dy + S, S), lax.rem(self.x + dx + S, S)
            view = piece(*self.at(*place))
            return view, view, self.send.at[self.base + n], self.recv.at[self.base + n], (self.r, y * S + x)
        return Copy(make)

    def at(self, dy, dx, part):
        y = None if dy is None else lax.rem(self.y + dy, S)
        x = None if dx is None else lax.rem(self.x + dx, S)
        return y, x, part

    def put(self, n, piece, place, dx, dy):
        copy = self.copy(n, piece, place, dx, dy)
        copy.start()
        self.sends.append(copy)

    def got(self, n, piece, place):
        self.copy(n, piece, place, 0, 0).came()

    def a0(self):
        self.put(0, self.a, (0, 0, 0), 1, 0)
        self.put(1, self.a, (0, 0, 0), -1, 0)
        self.put(2, self.b, (0, 0, 0), 0, 1)
        self.put(3, self.b, (0, 0, 0), 0, -1)

    def a1(self):
        self.got(0, self.a, (0, 3, 0))
        self.put(4, self.a, (0, 3, 1), 1, 0)
        self.got(2, self.b, (3, 0, 0))
        self.put(6, self.b, (3, 0, 1), 0, 1)
        self.got(1, self.a, (0, 1, 0))
        self.put(5, self.a, (0, 1, 2), -1, 0)
        self.got(3, self.b, (1, 0, 0))
        self.put(7, self.b, (1, 0, 2), 0, -1)

    def b0(self):
        self.got(4, self.a, (0, 2, 1))
        self.got(5, self.a, (0, 2, 2))
        self.put(8, self.a, (0, None, 0), 0, 1)
        self.put(9, self.a, (0, None, 0), 0, -1)
        self.got(6, self.b, (2, 0, 1))
        self.got(7, self.b, (2, 0, 2))
        self.put(10, self.b, (None, 0, 0), 1, 0)
        self.put(11, self.b, (None, 0, 0), -1, 0)

    def b1(self):
        self.got(8, self.a, (3, None, 0))
        self.put(12, self.a, (3, None, 1), 0, 1)
        self.got(10, self.b, (None, 3, 0))
        self.put(14, self.b, (None, 3, 1), 1, 0)
        self.got(9, self.a, (1, None, 0))
        self.put(13, self.a, (1, None, 2), 0, -1)
        self.got(11, self.b, (None, 1, 0))
        self.put(15, self.b, (None, 1, 2), -1, 0)

    def end(self):
        self.got(12, self.a, (2, None, 1))
        self.got(13, self.a, (2, None, 2))
        self.got(14, self.b, (None, 2, 1))
        self.got(15, self.b, (None, 2, 2))

    def sent(self):
        for copy in self.sends:
            copy.sent()


class Panel(Plane):
    def cut0(self, d):
        if d == 2:
            self.got(4, self.a, (0, 2, 1))
            self.got(5, self.a, (0, 2, 2))
            self.got(6, self.b, (2, 0, 1))
            self.got(7, self.b, (2, 0, 2))
        n = 8 + 8 * d
        self.put(n, self.a, (0, d, 0), 0, 1)
        self.put(n + 1, self.a, (0, d, 0), 0, -1)
        self.put(n + 2, self.b, (d, 0, 0), 1, 0)
        self.put(n + 3, self.b, (d, 0, 0), -1, 0)

    def cut1(self, d):
        n = 8 + 8 * d
        self.got(n, self.a, (3, d, 0))
        self.put(n + 4, self.a, (3, d, 1), 0, 1)
        self.got(n + 2, self.b, (d, 3, 0))
        self.put(n + 6, self.b, (d, 3, 1), 1, 0)
        self.got(n + 1, self.a, (1, d, 0))
        self.put(n + 5, self.a, (1, d, 2), 0, -1)
        self.got(n + 3, self.b, (d, 1, 0))
        self.put(n + 7, self.b, (d, 1, 2), -1, 0)

    def end(self):
        for d in (0, 1, 3, 2):
            n = 8 + 8 * d
            self.got(n + 4, self.a, (2, d, 1))
            self.got(n + 5, self.a, (2, d, 2))
            self.got(n + 6, self.b, (d, 2, 1))
            self.got(n + 7, self.b, (d, 2, 2))


class Gather:
    def __init__(self, z, q, c, buf, send, recv):
        self.z, self.q, self.c, self.buf, self.send, self.recv = z, q, c, buf, send, recv
        self.sends = []

    def copy(self, n, chunk, dz):
        def make():
            to = lax.rem(self.z + dz + Z, Z)
            view = self.buf.at[lax.rem(self.z + chunk + Z, Z)]
            return view, view, self.send.at[n], self.recv.at[n], (to * 2 + self.q, self.c)
        return Copy(make)

    def put(self, n, chunk, dz):
        copy = self.copy(n, chunk, dz)
        copy.start()
        self.sends.append(copy)

    def got(self, n, chunk):
        self.copy(n, chunk, 0).came()

    def first(self):
        self.put(0, 0, 2)
        self.put(8, 0, -2)
        self.put(4, 0, 1)
        self.put(11, 0, -1)

    def step(self, k):
        self.got(k - 1, -2 * k)
        self.put(k, -2 * k, 2)
        self.put(4 + k, -2 * k, 1)
        self.got(8 + k - 1, 2 * k)
        if k < 3:
            self.put(8 + k, 2 * k, -2)
        self.put(11 + k, 2 * k, -1)

    def end(self):
        self.got(3, -8)
        for k in range(4):
            self.got(4 + k, -2 * k - 1)
            self.got(11 + k, 2 * k + 1)

    def sent(self):
        for copy in self.sends:
            copy.sent()


class Spread:
    def __init__(self, z, q, c, buf, send, recv, k):
        self.z, self.q, self.c, self.buf, self.send, self.recv, self.k = z, q, c, buf, send, recv, k
        self.sends = []

    def copy(self, n, chunk, dz, m):
        def make():
            to = lax.rem(self.z + dz + Z, Z)
            view = self.buf.at[self.k, lax.rem(self.z + chunk + Z, Z)]
            n_, m_ = n + 16 * self.k, m + 16 * self.k
            return view, view, self.send.at[n_], self.recv.at[m_], (to * 2 + self.q, self.c)
        return Copy(make)

    def put(self, n, chunk, dz):
        away = dz - chunk
        copy = self.copy(n, chunk, dz, away - 1 if away > 0 else 7 - away)
        copy.start()
        self.sends.append(copy)

    def got(self, away):
        self.copy(0, -away, 0, away - 1 if away > 0 else 7 - away).came()

    def first(self):
        for n, d in enumerate((4, -4, 3, -3, 2, -2, 1, -1)):
            self.put(n, 0, d)

    def relay(self):
        self.got(4)
        for n, d in enumerate((4, 3, 2, 1)):
            self.put(8 + n, -4, d)
        self.got(-4)
        for n, d in enumerate((3, 2, 1)):
            self.put(12 + n, 4, -d)

    def end(self):
        for d in (1, 2, 3, 5, 6, 7, 8):
            self.got(d)
        for d in (1, 2, 3, 5, 6, 7):
            self.got(-d)

    def sent(self):
        for copy in self.sends:
            copy.sent()


class Reduce:
    def __init__(self, z, q, c, mine, slots, send, recv):
        self.z, self.q, self.c, self.mine, self.slots, self.send, self.recv = z, q, c, mine, slots, send, recv
        self.sends = []

    def put(self, n, d, dz, slot, i):
        def make():
            to = lax.rem(self.z + dz + Z, Z)
            return self.mine.at[d % Z], self.slots[slot].at[i], self.send.at[n], self.recv.at[n], (to * 2 + self.q, self.c)
        copy = Copy(make)
        copy.start()
        self.sends.append(copy)

    def got(self, n, slot, i):
        view = lambda: self.slots[slot].at[i]
        Copy(lambda: (view(), view(), self.send.at[n], self.recv.at[n], (self.z * 2 + self.q, self.c))).came()
        return self.slots[slot][i]

    def first(self):
        self.put(0, 8, 2, 0, 0)
        self.put(4, 7, 1, 1, 0)
        self.put(11, -7, -1, 3, 0)

    def rest(self):
        for i, d in ((1, 5), (2, 3), (3, 1)):
            self.put(4 + i, d, 1, 1, i)
            self.put(11 + i, -d, -1, 3, i)

    def left(self):
        self.mine[10] += self.got(11, 3, 0)
        self.put(8, -6, -2, 2, 0)

    def round(self, k):
        d = 8 - 2 * k
        one = self.got(k - 1, 0, k - 1)
        self.mine[d] += one + self.got(4 + k - 1, 1, k - 1)
        self.put(k, d, 2, 0, k)
        if k < 3:
            d = 2 * k - 8 + 2
            one = self.got(8 + k - 1, 2, k - 1)
            self.mine[d % Z] += one + self.got(11 + k, 3, k)
            self.put(8 + k, d, -2, 2, k)

    def total(self):
        one = self.got(3, 0, 3) + self.got(7, 1, 3)
        two = self.got(10, 2, 2) + self.got(14, 3, 3)
        return self.mine[0] + (one + two)

    def sent(self):
        for copy in self.sends:
            copy.sent()


def kernel(
    slot_ref, flag_ref, rhs_ref, panel_ref, diag_ref, out_ref,
    full, mine0, other0, mine1, other1, minep, otherp, far_r, near_r, far_l, near_l, pfar_r, pnear_r, pfar_l, pnear_l,
    hop_r, hop_l, dz, ee, p10, b0, b1c, b1, chunk1, x0, x1, xh, xl,
    p_send, p_recv, e_send, e_recv, t_send, t_recv, r0_send, r0_recv, g0_send, g0_recv, y_send, y_recv,
    r1_send, r1_recv, rp_send, rp_recv, g1_send, g1_recv, gd_send, gd_recv, m_send, m_recv, f_send, f_recv,
):
    r, c = lax.axis_index("row"), lax.axis_index("col")
    z, q = r // 2, lax.rem(r, 2)
    y, x = c // S, lax.rem(c, S)
    pair = (z * 2 + 1 - q, c)

    def turn(a, n):
        return lax.rem(a + 2 * n, n)

    barrier = pltpu.get_barrier_semaphore()

    def hello(device):
        pl.semaphore_signal(barrier, inc=1, device_id=device, device_id_type=MESH)

    for dy, dx in ((0, 1), (0, -1), (1, 0), (-1, 0)):
        hello((r, turn(y + dy, S) * S + turn(x + dx, S)))
    hello(pair)
    for dist in (1, -1, 2, -2):
        hello((turn(z + dist, Z) * 2 + q, c))

    @pl.when(q == 0)
    def _():
        for dist in (3, -3, 4, -4):
            hello((lax.rem(z + dist + Z, Z) * 2, c))

    held = slot_ref[r]
    is0 = jnp.where(held == 0, 1.0, 0.0).astype(F32)
    is1 = jnp.where(held == 1, 1.0, 0.0).astype(F32)
    f0 = flag_ref[0, 0].astype(F32)
    f1 = flag_ref[0, 1].astype(F32)

    def keep(mark, a, b):
        return jnp.where(jnp.full(a.shape, mark, F32) > 0.5, a, b)

    def mask0(d, _):
        j = lax.rem(z + d, Z)
        rows = rhs_ref[j // 4, lax.rem(j, 4)]
        mine0[d] = keep(is0, rows, jnp.zeros_like(rows))
        return 0

    def mask1(d, _):
        j = lax.rem(z + d, Z)
        t, h = j // 2, lax.rem(j, 2)
        block = panel_ref[0, pl.ds(pl.multiple_of(t * 8, 8), 8), :] * f0
        minep[d] = keep(is1, block, jnp.zeros_like(block))
        for k in range(16):
            rows = rhs_ref[k // 4, k % 4, pl.ds(pl.multiple_of(t * 8, 8), 8), pl.ds(pl.multiple_of(h * 128, 128), 128)]
            mine1[d, 8 * k : 8 * k + 8, :] = keep(is1, rows, jnp.zeros_like(rows))
        return 0

    lax.fori_loop(0, Z, mask0, 0)
    lax.fori_loop(0, Z, mask1, 0)
    for k in range(2):
        full[k, y, x] = panel_ref[k]

    @pl.when(q == 0)
    def _():
        pl.semaphore_wait(barrier, 13)

    @pl.when(q == 1)
    def _():
        pl.semaphore_wait(barrier, 9)

    place = (r, y, x)

    def half(lo, hi, k):
        def piece(yy, xx, part):
            mid = (lo + hi) // 2
            rows = pl.ds(*((lo, hi - lo), (lo, mid - lo), (mid, hi - mid))[part])
            yy = slice(None) if yy is None else yy
            xx = slice(None) if xx is None else xx
            return full.at[k, yy, xx, rows, :]
        return piece

    def columns(buf, lo, hi, k=None):
        def piece(yy, xx, part):
            mid = (lo + hi) // 2
            cols = pl.ds(*((lo, hi - lo), (lo, mid - lo), (mid, hi - mid))[part])
            yy = slice(None) if yy is None else yy
            xx = slice(None) if xx is None else xx
            return buf.at[yy, xx, :, cols] if k is None else buf.at[k, yy, xx, :, cols]
        return piece

    def planes():
        return [Panel(place, half(0, 32, k), half(32, 64, k), p_send, p_recv, 40 * k) for k in range(2)]

    diags = [Plane(place, columns(ee, 0, 2560, k), columns(ee, 2560, 5120, k), e_send, e_recv, 16 * k) for k in range(2)]
    tenth = Plane(place, columns(p10, 0, 512), columns(p10, 512, 1024), t_send, t_recv)
    reduce0 = Reduce(z, q, c, mine0, (far_r, near_r, far_l, near_l), r0_send, r0_recv)
    reducep = Reduce(z, q, c, minep, (pfar_r, pnear_r, pfar_l, pnear_l), rp_send, rp_recv)
    gather0 = Gather(z, q, c, b0, g0_send, g0_recv)
    gather1 = Gather(z, q, c, b1c, g1_send, g1_recv)
    spreads = [Spread(z, q, c, dz, gd_send, gd_recv, k) for k in range(2)]

    def give(n, src, dst, send=f_send, recv=f_recv):
        return Copy(lambda: (src(), dst(), send.at[n], recv.at[n], pair))

    groups = ((6, 5), (11, 5), (0, 6))
    merges = [
        give(i, lambda g=g: mine0.at[pl.ds(*g)], lambda g=g: other0.at[pl.ds(*g)], m_send, m_recv)
        for i, g in enumerate(groups)
    ]
    mergep = give(3, lambda: minep, lambda: otherp, m_send, m_recv)
    merge1 = give(4, lambda: mine1, lambda: other1, m_send, m_recv)
    owner = c // 8

    def diag_piece():
        first_row = pl.multiple_of(lax.rem(c // 2, 4) * 8, 8)
        first_col = pl.multiple_of(lax.rem(c, 2) * (z // 4 + 1) * 128, 128)
        return slice(None), pl.ds(first_row, 8), pl.ds(first_col, 512)

    give_dz = give(1, lambda: diag_ref.at[diag_piece()], lambda: dz.at[:, z])
    give_p10 = give(2, lambda: p10, lambda: p10)
    give_chunk = give(3, lambda: mine1.at[0], lambda: chunk1)

    def give_rows(k, d):
        a = lambda: ee.at[k, lax.rem(y + d, S), :, :, 0:2560]
        b = lambda: ee.at[k, :, lax.rem(x + d, S), :, 2560:5120]
        return [give(8 * k + 2 * d, a, a, y_send, y_recv), give(8 * k + 2 * d + 1, b, b, y_send, y_recv)]

    give_ee = [sum((give_rows(k, d) for d in range(S)), []) for k in range(2)]
    give_x0 = give(5, lambda: x0, lambda: x0)
    give_x1 = [give(6 + i, lambda i=i: x1.at[i], lambda i=i: x1.at[i]) for i in range(4)]

    sums1 = []

    def hop(t):
        def put(n, d, dz_, buf, i):
            copy = Copy(lambda: (mine1.at[d % Z], buf.at[i], r1_send.at[n], r1_recv.at[n], (turn(z + dz_, Z) * 2 + q, c)))
            copy.start()
            sums1.append(copy)

        def got(n, buf, i):
            Copy(lambda: (buf.at[i], buf.at[i], r1_send.at[n], r1_recv.at[n], (r, c))).came()
            return buf[i]

        if t:
            mine1[8 - t] += got(t - 1, hop_r, t - 1)
        if t < 8:
            put(t, 8 - t, 1, hop_r, t)
        if 0 < t < 8:
            mine1[(t - 7) % Z] += got(8 + t - 1, hop_l, t - 1)
        if t < 7:
            put(8 + t, t - 7, -1, hop_l, t)

    def take(load, n):
        for i in range(1024 // n):
            high, low_part = split(load(i))
            xh[n * i : n * i + n, :] = high
            xl[n * i : n * i + n, :] = low_part

    def unit(d, load):
        top_rows = load(lax.rem(y + d, S), slice(None), slice(0, 32))
        bottom_rows = load(slice(None), lax.rem(x + d, S), slice(32, 64))
        return jnp.concatenate([v.reshape(128, v.shape[-1]) for v in (top_rows, bottom_rows)], axis=0)

    def store(d, value):
        out_ref[lax.rem(y + d, S), :, 0:32, :] = value[:128].reshape(4, 32, 256)
        out_ref[:, lax.rem(x + d, S), 32:64, :] = value[128:].reshape(4, 32, 256)

    def product(k, d):
        return dot3(unit(d, lambda *at: full[(k, *at, slice(None))]), xh[...], xl[...])

    def step0(d):
        store(d, unit(d, lambda *at: rhs_ref[(*at, slice(None))]) - f0 * product(0, d))

    def step1(d):
        value = unit(d, lambda *at: out_ref[(*at, slice(None))]) - f1 * product(1, d)
        solved0 = unit(d, lambda *at: x0[(*at, slice(None))])
        solved1 = unit(d, lambda *at: x1[(*at, slice(None))])
        store(d, keep(is0, solved0, keep(is1, solved1, value)))

    def solve(k, done):
        off = 0
        for g in range(4):
            width = 128 * (g + 1)
            value = None
            for side in range(2):
                rows_ = []
                for i in range(4):
                    parts = [ee[k, :, 2 * o + side, :, off + width * i : off + width * i + width] for o in range(2)]
                    rows_.append(jnp.stack(parts, axis=1).reshape(64, width))
                lo = width * side
                term = dot3(jnp.concatenate(rows_, axis=0), xh[lo : lo + width, :], xl[lo : lo + width, :])
                value = term if value is None else value + term
            off += 4 * width
            done(g, value.reshape(4, 64, 256))

    @pl.when(q == 1)
    def _():
        panels = planes()
        panels[0].a0()
        mergep.start()

        @pl.when(owner == 1)
        def _():
            give_dz.start()

        merge1.start()
        panels[1].a0()

        def merge(i):
            merges[i].came()
            lo, n = groups[i]
            for d in range(lo, lo + n):
                mine0[d] += other0[d]

        merge(0)
        reduce0.first()
        merge(1)
        merge(2)
        reduce0.rest()
        reduce0.left()
        reduce0.round(1)
        panels[0].a1()
        panels[1].a1()
        reduce0.round(2)
        panels[0].cut0(0)
        reduce0.round(3)
        panels[0].cut0(1)
        b0[z] = reduce0.total()
        gather0.first()
        panels[0].cut0(3)
        gather0.step(1)
        panels[0].cut0(2)
        gather0.step(2)
        panels[0].cut1(0)
        panels[1].cut0(0)
        gather0.step(3)
        panels[0].cut1(1)
        panels[1].cut0(1)
        gather0.end()
        take(lambda i: b0[i], 64)
        for copy in give_ee[0]:
            copy.came()

        def done0(g, value):
            x0[g] = value

        solve(0, done0)
        give_x0.start()
        take(lambda i: x0[i].reshape(256, 256), 256)
        panels[0].cut1(3)
        panels[1].cut0(3)
        give_p10.came()
        give_chunk.came()
        h = pl.multiple_of(lax.rem(z, 2) * 128, 128)
        b1c[z] = chunk1[...] - dot3(p10[...].reshape(128, 1024), xh[:, pl.ds(h, 128)], xl[:, pl.ds(h, 128)])
        gather1.first()
        panels[0].cut1(2)
        panels[1].cut0(2)
        step0(0)
        gather1.step(1)
        panels[1].cut1(0)
        step0(1)
        gather1.step(2)
        panels[1].cut1(1)
        step0(3)
        gather1.step(3)
        panels[1].cut1(3)
        panels[0].end()
        step0(2)
        gather1.end()
        for t in range(8):
            for h in range(2):
                for k in range(16):
                    b1[64 * k + 8 * t : 64 * k + 8 * t + 8, 128 * h : 128 * h + 128] = b1c[2 * t + h, 8 * k : 8 * k + 8, :]
        take(lambda i: b1[256 * i : 256 * i + 256, :], 256)
        panels[1].cut1(2)
        for copy in give_ee[1]:
            copy.came()

        def done1(g, value):
            x1[g] = value
            give_x1[g].start()

        solve(1, done1)
        take(lambda i: x1[i].reshape(256, 256), 256)
        for d in (0, 1, 3):
            step1(d)
        panels[1].end()
        step1(2)
        for part in panels + [reduce0, gather0, gather1]:
            part.sent()
        for copy in [mergep, merge1, give_x0] + give_x1:
            copy.sent()

        @pl.when(owner == 1)
        def _():
            give_dz.sent()

    @pl.when(q == 0)
    def _():
        panels = planes()

        def pack(k):
            off = 0
            for i in range(16):
                width = 128 * (i // 4 + 1)
                ee[k, y, x, :, off : off + width] = dz[k, i, :, 0:width]
                off += width

        def hand(k, *distances):
            for d in distances:
                for copy in give_ee[k][2 * d : 2 * d + 2]:
                    copy.start()

        for copy in merges:
            copy.start()

        @pl.when(owner == 0)
        def _():
            dz[:, z] = diag_ref[diag_piece()]

        @pl.when(owner == 1)
        def _():
            give_dz.came()

        spreads[0].first()
        panels[0].a0()
        mergep.came()
        minep[...] += otherp[...]
        reducep.first()
        reducep.rest()
        panels[1].a0()
        merge1.came()
        mine1[...] += other1[...]
        hop(0)
        reducep.left()
        spreads[0].relay()
        reducep.round(1)
        panels[0].a1()
        hop(1)
        panels[1].a1()
        spreads[0].end()
        pack(0)
        diags[0].a0()
        reducep.round(2)
        hop(2)
        panels[0].cut0(0)
        diags[0].a1()
        reducep.round(3)
        hop(3)
        spreads[1].first()
        panels[0].cut0(1)
        diags[0].b0()
        p10[y, x] = reducep.total()
        tenth.a0()
        hop(4)
        panels[0].cut0(3)
        spreads[1].relay()
        tenth.a1()
        diags[0].b1()
        hand(0, 0, 1, 3)
        hop(5)
        panels[0].cut0(2)
        tenth.b0()
        diags[0].end()
        hand(0, 2)
        hop(6)
        spreads[1].end()
        pack(1)
        diags[1].a0()
        panels[0].cut1(0)
        panels[1].cut0(0)
        tenth.b1()
        hop(7)
        diags[1].a1()
        panels[0].cut1(1)
        panels[1].cut0(1)
        tenth.end()
        give_p10.start()
        hop(8)
        give_chunk.start()
        diags[1].b0()
        panels[0].cut1(3)
        panels[1].cut0(3)
        diags[1].b1()
        hand(1, 0, 1, 3)
        panels[0].cut1(2)
        panels[1].cut0(2)
        panels[1].cut1(0)
        diags[1].end()
        hand(1, 2)
        give_x0.came()
        take(lambda i: x0[i].reshape(256, 256), 256)
        step0(0)
        panels[1].cut1(1)
        step0(1)
        panels[1].cut1(3)
        step0(3)
        panels[1].cut1(2)
        panels[0].end()
        step0(2)
        for copy in give_x1:
            copy.came()
        take(lambda i: x1[i].reshape(256, 256), 256)
        for d in (0, 1, 3):
            step1(d)
        panels[1].end()
        step1(2)
        for part in panels + diags + spreads + [reducep, tenth]:
            part.sent()
        for copy in merges + sums1 + give_ee[0] + give_ee[1] + [give_p10, give_chunk]:
            copy.sent()


def shards(rhs, panel, diag_inverse, flags, slot_block):
    vmem = lambda *shape, dtype=F32: pltpu.VMEM(shape, dtype)
    dma = lambda *shape: pltpu.SemaphoreType.DMA(shape)
    scratch = [
        vmem(2, 4, 4, 64, 1024),
        vmem(16, 64, 256), vmem(16, 64, 256),
        vmem(16, 128, 128), vmem(16, 128, 128),
        vmem(16, 8, 1024), vmem(16, 8, 1024),
        vmem(4, 64, 256), vmem(4, 64, 256), vmem(3, 64, 256), vmem(4, 64, 256),
        vmem(4, 8, 1024), vmem(4, 8, 1024), vmem(3, 8, 1024), vmem(4, 8, 1024),
        vmem(8, 128, 128), vmem(7, 128, 128),
        vmem(2, 16, 8, 512),
        vmem(2, 4, 4, 8, 5120),
        vmem(4, 4, 8, 1024),
        vmem(16, 64, 256),
        vmem(16, 128, 128),
        vmem(1024, 256),
        vmem(128, 128),
        vmem(4, 4, 64, 256),
        vmem(4, 4, 64, 256),
        vmem(1024, 256, dtype=BF16), vmem(1024, 256, dtype=BF16),
        dma(80), dma(80), dma(32), dma(32),
    ]
    scratch += [dma(16) for _ in range(14)]
    scratch += [dma(32), dma(32)]
    scratch += [dma(5), dma(5), dma(10), dma(10)]
    whole = pl.BlockSpec(memory_space=pltpu.VMEM)
    scalar = pl.BlockSpec(memory_space=pltpu.SMEM)
    result = pl.pallas_call(
        kernel,
        out_shape=jax.ShapeDtypeStruct((4, 4, 64, 256), F32),
        in_specs=[scalar, scalar, whole, whole, whole],
        out_specs=whole,
        scratch_shapes=scratch,
        name="substitution",
        compiler_params=pltpu.CompilerParams(collective_id=0, has_side_effects=True, vmem_limit_bytes=56 << 20),
    )(slot_block, flags, rhs.reshape(4, 4, 64, 256), panel[0], diag_inverse)
    return result.reshape(1, 1024, 256)


def solution(mesh):
    in_specs = (
        P("row", None, "col"),
        P("row", None, "col", None),
        P(None, "row", None),
        P("row", None),
        P(),
    )
    out_specs = P("row", None, "col")
    return jax.shard_map(shards, mesh=mesh, in_specs=in_specs, out_specs=out_specs, check_vma=False)
```

```python
import jax
import jax.numpy as jnp
from jax import lax
from jax.experimental import pallas as pl
from jax.experimental.pallas import tpu as pltpu
from jax.sharding import PartitionSpec as P

MESH = pl.DeviceIdType.MESH
F32 = jnp.float32
BF16 = jnp.bfloat16
Z = 16
S = 4


def split(a):
    high = a.astype(BF16)
    return high, (a - high.astype(F32)).astype(BF16)


def dot(a, b):
    return jnp.dot(a, b, preferred_element_type=F32)


def dot3(a, b_high, b_low):
    a_high, a_low = split(a)
    return dot(a_high, b_high) + (dot(a_high, b_low) + dot(a_low, b_high))


class Copy:
    def __init__(self, make):
        self.make = make

    def op(self):
        src, dst, send, recv, device = self.make()
        return pltpu.make_async_remote_copy(
            src_ref=src, dst_ref=dst, send_sem=send, recv_sem=recv, device_id=device, device_id_type=MESH
        )

    def start(self):
        self.op().start()

    def sent(self):
        self.op().wait_send()

    def came(self):
        self.op().wait_recv()


class Plane:
    def __init__(self, place, a, b, send, recv, base=0):
        self.r, self.y, self.x = place
        self.a, self.b, self.send, self.recv, self.base = a, b, send, recv, base
        self.sends = []

    def copy(self, n, piece, place, dx, dy):
        def make():
            y, x = lax.rem(self.y + dy + S, S), lax.rem(self.x + dx + S, S)
            view = piece(*self.at(*place))
            return view, view, self.send.at[self.base + n], self.recv.at[self.base + n], (self.r, y * S + x)
        return Copy(make)

    def at(self, dy, dx, part):
        y = None if dy is None else lax.rem(self.y + dy, S)
        x = None if dx is None else lax.rem(self.x + dx, S)
        return y, x, part

    def put(self, n, piece, place, dx, dy):
        copy = self.copy(n, piece, place, dx, dy)
        copy.start()
        self.sends.append(copy)

    def got(self, n, piece, place):
        self.copy(n, piece, place, 0, 0).came()

    def a0(self):
        self.put(0, self.a, (0, 0, 0), 1, 0)
        self.put(1, self.a, (0, 0, 0), -1, 0)
        self.put(2, self.b, (0, 0, 0), 0, 1)
        self.put(3, self.b, (0, 0, 0), 0, -1)

    def a1(self):
        self.got(0, self.a, (0, 3, 0))
        self.put(4, self.a, (0, 3, 1), 1, 0)
        self.got(2, self.b, (3, 0, 0))
        self.put(6, self.b, (3, 0, 1), 0, 1)
        self.got(1, self.a, (0, 1, 0))
        self.put(5, self.a, (0, 1, 2), -1, 0)
        self.got(3, self.b, (1, 0, 0))
        self.put(7, self.b, (1, 0, 2), 0, -1)

    def b0(self):
        self.got(4, self.a, (0, 2, 1))
        self.got(5, self.a, (0, 2, 2))
        self.put(8, self.a, (0, None, 0), 0, 1)
        self.put(9, self.a, (0, None, 0), 0, -1)
        self.got(6, self.b, (2, 0, 1))
        self.got(7, self.b, (2, 0, 2))
        self.put(10, self.b, (None, 0, 0), 1, 0)
        self.put(11, self.b, (None, 0, 0), -1, 0)

    def b1(self):
        self.got(8, self.a, (3, None, 0))
        self.put(12, self.a, (3, None, 1), 0, 1)
        self.got(10, self.b, (None, 3, 0))
        self.put(14, self.b, (None, 3, 1), 1, 0)
        self.got(9, self.a, (1, None, 0))
        self.put(13, self.a, (1, None, 2), 0, -1)
        self.got(11, self.b, (None, 1, 0))
        self.put(15, self.b, (None, 1, 2), -1, 0)

    def end(self):
        self.got(12, self.a, (2, None, 1))
        self.got(13, self.a, (2, None, 2))
        self.got(14, self.b, (None, 2, 1))
        self.got(15, self.b, (None, 2, 2))

    def sent(self):
        for copy in self.sends:
            copy.sent()


class Panel(Plane):
    def cut0(self, d):
        if d == 2:
            self.got(4, self.a, (0, 2, 1))
            self.got(5, self.a, (0, 2, 2))
            self.got(6, self.b, (2, 0, 1))
            self.got(7, self.b, (2, 0, 2))
        n = 8 + 8 * d
        self.put(n, self.a, (0, d, 0), 0, 1)
        self.put(n + 1, self.a, (0, d, 0), 0, -1)
        self.put(n + 2, self.b, (d, 0, 0), 1, 0)
        self.put(n + 3, self.b, (d, 0, 0), -1, 0)

    def cut1(self, d):
        n = 8 + 8 * d
        self.got(n, self.a, (3, d, 0))
        self.put(n + 4, self.a, (3, d, 1), 0, 1)
        self.got(n + 2, self.b, (d, 3, 0))
        self.put(n + 6, self.b, (d, 3, 1), 1, 0)
        self.got(n + 1, self.a, (1, d, 0))
        self.put(n + 5, self.a, (1, d, 2), 0, -1)
        self.got(n + 3, self.b, (d, 1, 0))
        self.put(n + 7, self.b, (d, 1, 2), -1, 0)

    def end(self):
        for d in (0, 1, 3, 2):
            n = 8 + 8 * d
            self.got(n + 4, self.a, (2, d, 1))
            self.got(n + 5, self.a, (2, d, 2))
            self.got(n + 6, self.b, (d, 2, 1))
            self.got(n + 7, self.b, (d, 2, 2))


class Gather:
    def __init__(self, z, q, c, buf, send, recv):
        self.z, self.q, self.c, self.buf, self.send, self.recv = z, q, c, buf, send, recv
        self.sends = []

    def copy(self, n, chunk, dz):
        def make():
            to = lax.rem(self.z + dz + Z, Z)
            view = self.buf.at[lax.rem(self.z + chunk + Z, Z)]
            return view, view, self.send.at[n], self.recv.at[n], (to * 2 + self.q, self.c)
        return Copy(make)

    def put(self, n, chunk, dz):
        copy = self.copy(n, chunk, dz)
        copy.start()
        self.sends.append(copy)

    def got(self, n, chunk):
        self.copy(n, chunk, 0).came()

    def first(self):
        self.put(0, 0, 2)
        self.put(8, 0, -2)
        self.put(4, 0, 1)
        self.put(11, 0, -1)

    def step(self, k):
        self.got(k - 1, -2 * k)
        self.put(k, -2 * k, 2)
        self.put(4 + k, -2 * k, 1)
        self.got(8 + k - 1, 2 * k)
        if k < 3:
            self.put(8 + k, 2 * k, -2)
        self.put(11 + k, 2 * k, -1)

    def end(self):
        self.got(3, -8)
        for k in range(4):
            self.got(4 + k, -2 * k - 1)
            self.got(11 + k, 2 * k + 1)

    def sent(self):
        for copy in self.sends:
            copy.sent()


class Spread:
    def __init__(self, z, q, c, buf, send, recv, k):
        self.z, self.q, self.c, self.buf, self.send, self.recv, self.k = z, q, c, buf, send, recv, k
        self.sends = []

    def copy(self, n, chunk, dz, m):
        def make():
            to = lax.rem(self.z + dz + Z, Z)
            view = self.buf.at[self.k, lax.rem(self.z + chunk + Z, Z)]
            n_, m_ = n + 16 * self.k, m + 16 * self.k
            return view, view, self.send.at[n_], self.recv.at[m_], (to * 2 + self.q, self.c)
        return Copy(make)

    def put(self, n, chunk, dz):
        away = dz - chunk
        copy = self.copy(n, chunk, dz, away - 1 if away > 0 else 7 - away)
        copy.start()
        self.sends.append(copy)

    def got(self, away):
        self.copy(0, -away, 0, away - 1 if away > 0 else 7 - away).came()

    def first(self):
        for n, d in enumerate((4, -4, 3, -3, 2, -2, 1, -1)):
            self.put(n, 0, d)

    def relay(self):
        self.got(4)
        for n, d in enumerate((4, 3, 2, 1)):
            self.put(8 + n, -4, d)
        self.got(-4)
        for n, d in enumerate((3, 2, 1)):
            self.put(12 + n, 4, -d)

    def end(self):
        for d in (1, 2, 3, 5, 6, 7, 8):
            self.got(d)
        for d in (1, 2, 3, 5, 6, 7):
            self.got(-d)

    def sent(self):
        for copy in self.sends:
            copy.sent()


class Reduce:
    def __init__(self, z, q, c, mine, slots, send, recv):
        self.z, self.q, self.c, self.mine, self.slots, self.send, self.recv = z, q, c, mine, slots, send, recv
        self.sends = []

    def put(self, n, d, dz, slot, i):
        def make():
            to = lax.rem(self.z + dz + Z, Z)
            return self.mine.at[d % Z], self.slots[slot].at[i], self.send.at[n], self.recv.at[n], (to * 2 + self.q, self.c)
        copy = Copy(make)
        copy.start()
        self.sends.append(copy)

    def got(self, n, slot, i):
        view = lambda: self.slots[slot].at[i]
        Copy(lambda: (view(), view(), self.send.at[n], self.recv.at[n], (self.z * 2 + self.q, self.c))).came()
        return self.slots[slot][i]

    def first(self):
        self.put(0, 8, 2, 0, 0)
        self.put(4, 7, 1, 1, 0)
        self.put(11, -7, -1, 3, 0)

    def rest(self):
        for i, d in ((1, 5), (2, 3), (3, 1)):
            self.put(4 + i, d, 1, 1, i)
            self.put(11 + i, -d, -1, 3, i)

    def left(self):
        self.mine[10] += self.got(11, 3, 0)
        self.put(8, -6, -2, 2, 0)

    def round(self, k):
        d = 8 - 2 * k
        one = self.got(k - 1, 0, k - 1)
        self.mine[d] += one + self.got(4 + k - 1, 1, k - 1)
        self.put(k, d, 2, 0, k)
        if k < 3:
            d = 2 * k - 8 + 2
            one = self.got(8 + k - 1, 2, k - 1)
            self.mine[d % Z] += one + self.got(11 + k, 3, k)
            self.put(8 + k, d, -2, 2, k)

    def total(self):
        one = self.got(3, 0, 3) + self.got(7, 1, 3)
        two = self.got(10, 2, 2) + self.got(14, 3, 3)
        return self.mine[0] + (one + two)

    def sent(self):
        for copy in self.sends:
            copy.sent()


def kernel(
    slot_ref, flag_ref, rhs_ref, panel_ref, diag_ref, out_ref,
    full, mine0, other0, mine1, other1, minep, otherp, far_r, near_r, far_l, near_l, pfar_r, pnear_r, pfar_l, pnear_l,
    hop_r, hop_l, dz, ee, p10, b0, b1c, b1, chunk1, x0, x1, xh, xl,
    p_send, p_recv, e_send, e_recv, t_send, t_recv, r0_send, r0_recv, g0_send, g0_recv, y_send, y_recv,
    r1_send, r1_recv, rp_send, rp_recv, g1_send, g1_recv, gd_send, gd_recv, m_send, m_recv, f_send, f_recv,
):
    r, c = lax.axis_index("row"), lax.axis_index("col")
    z, q = r // 2, lax.rem(r, 2)
    y, x = c // S, lax.rem(c, S)
    pair = (z * 2 + 1 - q, c)

    def turn(a, n):
        return lax.rem(a + 2 * n, n)

    barrier = pltpu.get_barrier_semaphore()

    def hello(device):
        pl.semaphore_signal(barrier, inc=1, device_id=device, device_id_type=MESH)

    for dy, dx in ((0, 1), (0, -1), (1, 0), (-1, 0)):
        hello((r, turn(y + dy, S) * S + turn(x + dx, S)))
    hello(pair)
    for dist in (1, -1, 2, -2):
        hello((turn(z + dist, Z) * 2 + q, c))

    @pl.when(q == 0)
    def _():
        for dist in (3, -3, 4, -4):
            hello((lax.rem(z + dist + Z, Z) * 2, c))

    held = slot_ref[r]
    is0 = jnp.where(held == 0, 1.0, 0.0).astype(F32)
    is1 = jnp.where(held == 1, 1.0, 0.0).astype(F32)
    f0 = flag_ref[0, 0].astype(F32)
    f1 = flag_ref[0, 1].astype(F32)

    def keep(mark, a, b):
        return jnp.where(jnp.full(a.shape, mark, F32) > 0.5, a, b)

    def mask0(d, _):
        j = lax.rem(z + d, Z)
        rows = rhs_ref[j // 4, lax.rem(j, 4)]
        mine0[d] = keep(is0, rows, jnp.zeros_like(rows))
        return 0

    def mask1(d, _):
        j = lax.rem(z + d, Z)
        t, h = j // 2, lax.rem(j, 2)
        block = panel_ref[0, pl.ds(pl.multiple_of(t * 8, 8), 8), :] * f0
        minep[d] = keep(is1, block, jnp.zeros_like(block))
        for k in range(16):
            rows = rhs_ref[k // 4, k % 4, pl.ds(pl.multiple_of(t * 8, 8), 8), pl.ds(pl.multiple_of(h * 128, 128), 128)]
            mine1[d, 8 * k : 8 * k + 8, :] = keep(is1, rows, jnp.zeros_like(rows))
        return 0

    lax.fori_loop(0, Z, mask0, 0)
    lax.fori_loop(0, Z, mask1, 0)
    for k in range(2):
        full[k, y, x] = panel_ref[k]

    @pl.when(q == 0)
    def _():
        pl.semaphore_wait(barrier, 13)

    @pl.when(q == 1)
    def _():
        pl.semaphore_wait(barrier, 9)

    place = (r, y, x)

    def half(lo, hi, k):
        def piece(yy, xx, part):
            mid = (lo + hi) // 2
            rows = pl.ds(*((lo, hi - lo), (lo, mid - lo), (mid, hi - mid))[part])
            yy = slice(None) if yy is None else yy
            xx = slice(None) if xx is None else xx
            return full.at[k, yy, xx, rows, :]
        return piece

    def columns(buf, lo, hi, k=None):
        def piece(yy, xx, part):
            mid = (lo + hi) // 2
            cols = pl.ds(*((lo, hi - lo), (lo, mid - lo), (mid, hi - mid))[part])
            yy = slice(None) if yy is None else yy
            xx = slice(None) if xx is None else xx
            return buf.at[yy, xx, :, cols] if k is None else buf.at[k, yy, xx, :, cols]
        return piece

    def planes():
        return [Panel(place, half(0, 32, k), half(32, 64, k), p_send, p_recv, 40 * k) for k in range(2)]

    diags = [Plane(place, columns(ee, 0, 2560, k), columns(ee, 2560, 5120, k), e_send, e_recv, 16 * k) for k in range(2)]
    tenth = Plane(place, columns(p10, 0, 512), columns(p10, 512, 1024), t_send, t_recv)
    reduce0 = Reduce(z, q, c, mine0, (far_r, near_r, far_l, near_l), r0_send, r0_recv)
    reducep = Reduce(z, q, c, minep, (pfar_r, pnear_r, pfar_l, pnear_l), rp_send, rp_recv)
    gather0 = Gather(z, q, c, b0, g0_send, g0_recv)
    gather1 = Gather(z, q, c, b1c, g1_send, g1_recv)
    spreads = [Spread(z, q, c, dz, gd_send, gd_recv, k) for k in range(2)]

    def give(n, src, dst, send=f_send, recv=f_recv):
        return Copy(lambda: (src(), dst(), send.at[n], recv.at[n], pair))

    groups = ((6, 5), (11, 5), (0, 6))
    merges = [
        give(i, lambda g=g: mine0.at[pl.ds(*g)], lambda g=g: other0.at[pl.ds(*g)], m_send, m_recv)
        for i, g in enumerate(groups)
    ]
    mergep = give(3, lambda: minep, lambda: otherp, m_send, m_recv)
    merge1 = give(4, lambda: mine1, lambda: other1, m_send, m_recv)
    owner = c // 8

    def diag_piece():
        first_row = pl.multiple_of(lax.rem(c // 2, 4) * 8, 8)
        first_col = pl.multiple_of(lax.rem(c, 2) * (z // 4 + 1) * 128, 128)
        return slice(None), pl.ds(first_row, 8), pl.ds(first_col, 512)

    give_dz = give(1, lambda: diag_ref.at[diag_piece()], lambda: dz.at[:, z])
    give_p10 = give(2, lambda: p10, lambda: p10)
    give_chunk = give(3, lambda: mine1.at[0], lambda: chunk1)

    def give_rows(k, d):
        a = lambda: ee.at[k, lax.rem(y + d, S), :, :, 0:2560]
        b = lambda: ee.at[k, :, lax.rem(x + d, S), :, 2560:5120]
        return [give(8 * k + 2 * d, a, a, y_send, y_recv), give(8 * k + 2 * d + 1, b, b, y_send, y_recv)]

    give_ee = [sum((give_rows(k, d) for d in range(S)), []) for k in range(2)]
    give_x0 = give(5, lambda: x0, lambda: x0)
    give_x1 = [give(6 + i, lambda i=i: x1.at[i], lambda i=i: x1.at[i]) for i in range(4)]

    sums1 = []

    def hop(t):
        def put(n, d, dz_, buf, i):
            copy = Copy(lambda: (mine1.at[d % Z], buf.at[i], r1_send.at[n], r1_recv.at[n], (turn(z + dz_, Z) * 2 + q, c)))
            copy.start()
            sums1.append(copy)

        def got(n, buf, i):
            Copy(lambda: (buf.at[i], buf.at[i], r1_send.at[n], r1_recv.at[n], (r, c))).came()
            return buf[i]

        if t:
            mine1[8 - t] += got(t - 1, hop_r, t - 1)
        if t < 8:
            put(t, 8 - t, 1, hop_r, t)
        if 0 < t < 8:
            mine1[(t - 7) % Z] += got(8 + t - 1, hop_l, t - 1)
        if t < 7:
            put(8 + t, t - 7, -1, hop_l, t)

    def take(load, n):
        for i in range(1024 // n):
            high, low_part = split(load(i))
            xh[n * i : n * i + n, :] = high
            xl[n * i : n * i + n, :] = low_part

    def unit(d, load):
        top_rows = load(lax.rem(y + d, S), slice(None), slice(0, 32))
        bottom_rows = load(slice(None), lax.rem(x + d, S), slice(32, 64))
        return jnp.concatenate([v.reshape(128, v.shape[-1]) for v in (top_rows, bottom_rows)], axis=0)

    def store(d, value):
        out_ref[lax.rem(y + d, S), :, 0:32, :] = value[:128].reshape(4, 32, 256)
        out_ref[:, lax.rem(x + d, S), 32:64, :] = value[128:].reshape(4, 32, 256)

    def product(k, d):
        return dot3(unit(d, lambda *at: full[(k, *at, slice(None))]), xh[...], xl[...])

    def step0(d):
        store(d, unit(d, lambda *at: rhs_ref[(*at, slice(None))]) - f0 * product(0, d))

    def step1(d):
        value = unit(d, lambda *at: out_ref[(*at, slice(None))]) - f1 * product(1, d)
        solved0 = unit(d, lambda *at: x0[(*at, slice(None))])
        solved1 = unit(d, lambda *at: x1[(*at, slice(None))])
        store(d, keep(is0, solved0, keep(is1, solved1, value)))

    def solve(k, done):
        off = 0
        for g in range(4):
            width = 128 * (g + 1)
            value = None
            for side in range(2):
                rows_ = []
                for i in range(4):
                    parts = [ee[k, :, 2 * o + side, :, off + width * i : off + width * i + width] for o in range(2)]
                    rows_.append(jnp.stack(parts, axis=1).reshape(64, width))
                lo = width * side
                term = dot3(jnp.concatenate(rows_, axis=0), xh[lo : lo + width, :], xl[lo : lo + width, :])
                value = term if value is None else value + term
            off += 4 * width
            done(g, value.reshape(4, 64, 256))

    @pl.when(q == 1)
    def _():
        panels = planes()
        panels[0].a0()
        mergep.start()

        @pl.when(owner == 1)
        def _():
            give_dz.start()

        merge1.start()
        panels[1].a0()

        def merge(i):
            merges[i].came()
            lo, n = groups[i]
            for d in range(lo, lo + n):
                mine0[d] += other0[d]

        merge(0)
        reduce0.first()
        merge(1)
        merge(2)
        reduce0.rest()
        reduce0.left()
        reduce0.round(1)
        panels[0].a1()
        panels[1].a1()
        reduce0.round(2)
        panels[0].cut0(0)
        reduce0.round(3)
        panels[0].cut0(1)
        b0[z] = reduce0.total()
        gather0.first()
        panels[0].cut0(3)
        gather0.step(1)
        panels[0].cut0(2)
        gather0.step(2)
        panels[0].cut1(0)
        panels[1].cut0(0)
        gather0.step(3)
        panels[0].cut1(1)
        panels[1].cut0(1)
        gather0.end()
        take(lambda i: b0[i], 64)
        for copy in give_ee[0]:
            copy.came()

        def done0(g, value):
            x0[g] = value

        solve(0, done0)
        give_x0.start()
        take(lambda i: x0[i].reshape(256, 256), 256)
        panels[0].cut1(3)
        panels[1].cut0(3)
        give_p10.came()
        give_chunk.came()
        h = pl.multiple_of(lax.rem(z, 2) * 128, 128)
        b1c[z] = chunk1[...] - dot3(p10[...].reshape(128, 1024), xh[:, pl.ds(h, 128)], xl[:, pl.ds(h, 128)])
        gather1.first()
        panels[0].cut1(2)
        panels[1].cut0(2)
        step0(0)
        gather1.step(1)
        panels[1].cut1(0)
        step0(1)
        gather1.step(2)
        panels[1].cut1(1)
        step0(3)
        gather1.step(3)
        panels[1].cut1(3)
        panels[0].end()
        step0(2)
        gather1.end()
        for t in range(8):
            for h in range(2):
                for k in range(16):
                    b1[64 * k + 8 * t : 64 * k + 8 * t + 8, 128 * h : 128 * h + 128] = b1c[2 * t + h, 8 * k : 8 * k + 8, :]
        take(lambda i: b1[256 * i : 256 * i + 256, :], 256)
        panels[1].cut1(2)
        for copy in give_ee[1]:
            copy.came()

        def done1(g, value):
            x1[g] = value
            give_x1[g].start()

        solve(1, done1)
        take(lambda i: x1[i].reshape(256, 256), 256)
        for d in (0, 1, 3):
            step1(d)
        panels[1].end()
        step1(2)
        for part in panels + [reduce0, gather0, gather1]:
            part.sent()
        for copy in [mergep, merge1, give_x0] + give_x1:
            copy.sent()

        @pl.when(owner == 1)
        def _():
            give_dz.sent()

    @pl.when(q == 0)
    def _():
        panels = planes()

        def pack(k):
            off = 0
            for i in range(16):
                width = 128 * (i // 4 + 1)
                ee[k, y, x, :, off : off + width] = dz[k, i, :, 0:width]
                off += width

        def hand(k, *distances):
            for d in distances:
                for copy in give_ee[k][2 * d : 2 * d + 2]:
                    copy.start()

        for copy in merges:
            copy.start()

        @pl.when(owner == 0)
        def _():
            dz[:, z] = diag_ref[diag_piece()]

        @pl.when(owner == 1)
        def _():
            give_dz.came()

        spreads[0].first()
        panels[0].a0()
        mergep.came()
        minep[...] += otherp[...]
        reducep.first()
        reducep.rest()
        panels[1].a0()
        merge1.came()
        mine1[...] += other1[...]
        hop(0)
        reducep.left()
        spreads[0].relay()
        reducep.round(1)
        panels[0].a1()
        hop(1)
        panels[1].a1()
        spreads[0].end()
        pack(0)
        diags[0].a0()
        reducep.round(2)
        hop(2)
        panels[0].cut0(0)
        diags[0].a1()
        reducep.round(3)
        hop(3)
        spreads[1].first()
        panels[0].cut0(1)
        diags[0].b0()
        p10[y, x] = reducep.total()
        tenth.a0()
        hop(4)
        panels[0].cut0(3)
        spreads[1].relay()
        tenth.a1()
        diags[0].b1()
        hand(0, 0, 1, 3)
        hop(5)
        panels[0].cut0(2)
        tenth.b0()
        diags[0].end()
        hand(0, 2)
        hop(6)
        spreads[1].end()
        pack(1)
        diags[1].a0()
        panels[0].cut1(0)
        panels[1].cut0(0)
        tenth.b1()
        hop(7)
        diags[1].a1()
        panels[0].cut1(1)
        panels[1].cut0(1)
        tenth.end()
        give_p10.start()
        hop(8)
        give_chunk.start()
        diags[1].b0()
        panels[0].cut1(3)
        panels[1].cut0(3)
        diags[1].b1()
        hand(1, 0, 1, 3)
        panels[0].cut1(2)
        panels[1].cut0(2)
        panels[1].cut1(0)
        diags[1].end()
        hand(1, 2)
        give_x0.came()
        take(lambda i: x0[i].reshape(256, 256), 256)
        step0(0)
        panels[1].cut1(1)
        step0(1)
        panels[1].cut1(3)
        step0(3)
        panels[1].cut1(2)
        panels[0].end()
        step0(2)
        for copy in give_x1:
            copy.came()
        take(lambda i: x1[i].reshape(256, 256), 256)
        for d in (0, 1, 3):
            step1(d)
        panels[1].end()
        step1(2)
        for part in panels + diags + spreads + [reducep, tenth]:
            part.sent()
        for copy in merges + sums1 + give_ee[0] + give_ee[1] + [give_p10, give_chunk]:
            copy.sent()


def hand_out(value_ref, result_ref):
    result_ref[...] = value_ref[...]


def shards(rhs, panel, diag_inverse, flags, slot_block):
    vmem = lambda *shape, dtype=F32: pltpu.VMEM(shape, dtype)
    dma = lambda *shape: pltpu.SemaphoreType.DMA(shape)
    scratch = [
        vmem(2, 4, 4, 64, 1024),
        vmem(16, 64, 256), vmem(16, 64, 256),
        vmem(16, 128, 128), vmem(16, 128, 128),
        vmem(16, 8, 1024), vmem(16, 8, 1024),
        vmem(4, 64, 256), vmem(4, 64, 256), vmem(3, 64, 256), vmem(4, 64, 256),
        vmem(4, 8, 1024), vmem(4, 8, 1024), vmem(3, 8, 1024), vmem(4, 8, 1024),
        vmem(8, 128, 128), vmem(7, 128, 128),
        vmem(2, 16, 8, 512),
        vmem(2, 4, 4, 8, 5120),
        vmem(4, 4, 8, 1024),
        vmem(16, 64, 256),
        vmem(16, 128, 128),
        vmem(1024, 256),
        vmem(128, 128),
        vmem(4, 4, 64, 256),
        vmem(4, 4, 64, 256),
        vmem(1024, 256, dtype=BF16), vmem(1024, 256, dtype=BF16),
        dma(80), dma(80), dma(32), dma(32),
    ]
    scratch += [dma(16) for _ in range(14)]
    scratch += [dma(32), dma(32)]
    scratch += [dma(5), dma(5), dma(10), dma(10)]
    whole = pl.BlockSpec(memory_space=pltpu.VMEM)
    scalar = pl.BlockSpec(memory_space=pltpu.SMEM)
    result = pl.pallas_call(
        kernel,
        out_shape=jax.ShapeDtypeStruct((4, 4, 64, 256), F32),
        in_specs=[scalar, scalar, whole, whole, whole],
        out_specs=whole,
        scratch_shapes=scratch,
        name="substitution",
        compiler_params=pltpu.CompilerParams(collective_id=0, has_side_effects=True, vmem_limit_bytes=56 << 20),
    )(slot_block, flags, rhs.reshape(4, 4, 64, 256), panel[0], diag_inverse)
    block = pl.BlockSpec((256, 256), lambda i: (i, 0))
    return pl.pallas_call(
        hand_out,
        grid=(4,),
        out_shape=jax.ShapeDtypeStruct((1024, 256), F32),
        in_specs=[block],
        out_specs=block,
        name="hand_out",
    )(result.reshape(1024, 256)).reshape(1, 1024, 256)


def solution(mesh):
    in_specs = (
        P("row", None, "col"),
        P("row", None, "col", None),
        P(None, "row", None),
        P("row", None),
        P(),
    )
    out_specs = P("row", None, "col")
    return jax.shard_map(shards, mesh=mesh, in_specs=in_specs, out_specs=out_specs, check_vma=False)
```
